32 devices in a mesh: grp: 2 (over y), row: 4 (over z), col: 2 (over x), freq: 2 (over core).
Axes of the slice: x: 2, y: 2, z: 4, core: 2. Of those that a mesh axis runs over, the one named last changes fastest.
Arguments:
- w_freq: bfloat16 [64, 288, 4096], P(('grp', 'freq'), 'row', 'col'), parts along dimension 0, may hold values from -6 to 6
- x_rows: bfloat16 [576, 2048], P(('grp', 'row')), parts along dimension 0, may hold values from -6 to 6
- x_cols: bfloat16 [8192, 2048], P(('grp', 'col', 'freq')), parts along dimension 0, may hold values from -6 to 6
- occupation: float32 [8, 2048], P('grp'), parts along dimension 0, may hold values from 0.05 to 1
Outputs:
- sigma_orb: float32 [8, 2048, 2048], P('grp', 'row', ('col', 'freq')), parts along dimension 0
The draws below stay inside these ranges and needn't reach their ends.
There are 2 independent parts, one for each index of `grp`. The reference program is written for one: setup_inputs(seed, part) draws one part's arguments, and reference() takes and returns one part's arrays. A program takes and returns all parts, laid end to end along the dimension named above; each array names one. Nothing has to cross between parts.
All inputs are finite; a program needn't handle non-finite values.
Results may differ from the reference program's by a relative error of at most 0.005.
Values may be sent and summed in bfloat16 or wider, within the bound.
A program may use at most 128 MiB of HBM per device.

```python
import math
import jax
import jax.numpy as jnp
from jax import lax

NORB = 2048
P_SIZE = 4096
NW = 32
NT = 4
ROWS = 288


def block_scale(rng, dims, split, low, high):
    def one(position, shards_of):
        heights = jax.random.uniform(jax.random.fold_in(jax.random.fold_in(rng, 6), position), (shards_of,), jnp.float32, low / len(split), high / len(split))
        return jnp.repeat(jnp.exp(heights), dims[position] // shards_of).reshape((-1,) + (1,) * (len(dims) - position - 1))

    factor_of = one(*split[0])
    for cut in split[1:]:
        factor_of = factor_of * one(*cut)
    return factor_of


def scatter_about(rng, extent, spread, most, shards=(), held_as=jnp.bfloat16):
    gain = block_scale(rng, extent, shards, -0.22, 0.18) if shards else 1.0
    drawn = jax.random.normal(rng, extent, jnp.float32) * spread * gain
    return jnp.minimum(jnp.maximum(drawn, -most), most).astype(held_as)


def setup_inputs(seed: int = 0, part: int = 0) -> dict:
    splits = jax.random.split(jax.random.key(seed), 5)
    own_keys = jax.random.split(jax.random.fold_in(splits[4], part), 5)
    w_freq = scatter_about(own_keys[0], (NW, ROWS, P_SIZE), 1.0, 6.0, ((0, 2), (1, 4), (2, 2)))
    x_rows = scatter_about(own_keys[1], (ROWS, NORB), 1.0, 6.0, ((0, 4),))
    x_cols = scatter_about(own_keys[2], (P_SIZE, NORB), 1.0, 6.0, ((0, 4),))
    occupation = jnp.clip(jnp.exp(jax.random.uniform(own_keys[3], (NT, NORB), jnp.float32, math.log(0.05), math.log(1.0))), 0.05, 1.0)
    return {"w_freq": w_freq, "x_rows": x_rows, "x_cols": x_cols, "occupation": occupation}


def bosonic_table(tau_count, freq_count):
    omega = jnp.arange(freq_count, dtype=jnp.float32)
    steps_tau = jnp.arange(tau_count, dtype=jnp.float32) + 1.0
    weights = jnp.where(omega == 0.0, 1.0, 2.0).astype(jnp.float32)
    phases = 2.0 * math.pi * steps_tau[:, None] * omega[None, :] / (tau_count + 1.0)
    return (weights[None, :] * jnp.cos(phases) / math.sqrt(2.0 * freq_count)).astype(jnp.float32)

def reference(w_freq, x_rows, x_cols, occupation):
    transform = bosonic_table(NT, NW)
    flattened = w_freq.reshape(NW, -1).astype(jnp.float32)
    w_tau = jnp.dot(transform, flattened, precision=lax.Precision.HIGHEST).reshape(NT, ROWS, P_SIZE)
    results = []
    for tau_step in range(NT):
        scaled = (x_rows.astype(jnp.float32) * occupation[tau_step][None, :]).astype(jnp.bfloat16)
        green_tau = jnp.dot(scaled, x_cols.T, preferred_element_type=jnp.float32) / math.sqrt(NORB)
        sigma_tau = (green_tau * w_tau[tau_step]).astype(jnp.bfloat16)
        half_proj = (jnp.dot(sigma_tau, x_cols, preferred_element_type=jnp.float32) / math.sqrt(P_SIZE)).astype(jnp.bfloat16)
        results.append(jnp.dot(x_rows.T, half_proj, preferred_element_type=jnp.float32) / math.sqrt(ROWS))
    return jnp.stack(results, axis=0)
```

```python
import functools
import math

import jax
import jax.numpy as jnp
from jax import lax
from jax.experimental import pallas as pl
from jax.experimental.pallas import tpu as pltpu
from jax.sharding import PartitionSpec as P

F32 = jnp.float32
BF16 = jnp.bfloat16
MESH = pl.DeviceIdType.MESH
CHUNK = 256
QBLOCK = 256


def remote(src, dst, send_sem, recv_sem, device):
    return pltpu.make_async_remote_copy(
        src_ref=src, dst_ref=dst, send_sem=send_sem, recv_sem=recv_sem,
        device_id=device, device_id_type=MESH,
    )


def coefficients(f, shards, per_shard, tau_count, extra):
    period = tau_count + 1
    norm = extra / math.sqrt(2.0 * shards * per_shard)

    def pick(values):
        out = jnp.float32(values[0])
        for s in range(1, shards):
            out = jnp.where(f == s, jnp.float32(values[s]), out)
        return out

    coef = [
        [
            pick([
                2.0 * norm * math.cos(2.0 * math.pi * (((a + 1) * (s * per_shard + m)) % period) / period)
                for s in range(shards)
            ])
            for m in range(period)
        ]
        for a in range(tau_count // 2)
    ]
    drop = pick([norm if s == 0 else 0.0 for s in range(shards)])
    return coef, drop


def gather_kernel(
    rows_axis, cols_axis, tau_count, x_rows, occ, w_hbm, xc_hbm, hp, rbt,
    wbuf, xc, wsend, wown, wrecv, scaled, sig, p_send, p_recv, keep, x_send, x_recv, rb,
    lsem, w_sem, p_ssem, p_rsem, x_ssem, x_rsem, b_ssem, b_rsem, z_ssem, z_rsem,
):
    R, C = rows_axis, cols_axis
    z, c, f = lax.axis_index("row"), lax.axis_index("col"), lax.axis_index("freq")
    pairs = tau_count // 2
    rows, norb = x_rows.shape
    per_shard = w_hbm.shape[0]
    Q = xc.shape[0]
    owned = norb // (2 * C)
    parts = owned // CHUNK
    n = pairs * parts
    win = rb.shape[2]
    ichunk = norb // R
    core = {"freq": 1 - f}

    loads = [
        pltpu.make_async_copy(w_hbm.at[:, :, pl.ds(pl.multiple_of((1 - f) * Q, 128), Q)], wbuf.at[0], lsem.at[0]),
        pltpu.make_async_copy(w_hbm.at[:, :, pl.ds(pl.multiple_of(f * Q, 128), Q)], wbuf.at[1], lsem.at[1]),
        pltpu.make_async_copy(xc_hbm, xc, lsem.at[2]),
    ]
    for load in loads:
        load.start()

    barrier = pltpu.get_barrier_semaphore()
    pl.semaphore_signal(barrier, inc=1, device_id=core, device_id_type=MESH)
    for s in range(1, C):
        pl.semaphore_signal(barrier, inc=1, device_id={"col": lax.rem(c + s, C)}, device_id_type=MESH)

    @pl.loop(1, R)
    def _(s):
        pl.semaphore_signal(barrier, inc=1, device_id={"row": lax.rem(z + s, R)}, device_id_type=MESH)

    pl.semaphore_wait(barrier, 1 + (C - 1) + (R - 1))

    def window(to):
        return pl.ds(pl.multiple_of((to * ichunk) // win * win, 128), win)

    def basis_copy(s):
        to = lax.rem(z + s, R)
        return remote(x_rows.at[:, window(to)], rb.at[z], b_ssem.at[s], b_rsem.at[s], {"row": to})

    def basis_arrival(s):
        return remote(
            x_rows.at[:, window(z)], rb.at[lax.rem(z - s + R, R)], b_ssem.at[s], b_rsem.at[s], {"row": lax.rem(z + s, R)}
        )

    @pl.loop(1, R)
    def _(s):
        basis_copy(s).start()

    own_basis = pltpu.make_async_copy(x_rows.at[:, window(z)], rb.at[z], lsem.at[3])
    own_basis.start()

    coef, drop = coefficients(f, 2, per_shard, tau_count, 1.0 / math.sqrt(norb))
    period = tau_count + 1

    def fold(src, dst):
        @pl.loop(0, Q // 128)
        def _(b):
            lanes = pl.ds(pl.multiple_of(b * 128, 128), 128)
            first = src[0, :, lanes].astype(F32)
            acc = [first * (-drop)] * pairs
            for m in range(period):
                total = first if m == 0 else src[m, :, lanes].astype(F32)
                for i in range(m + period, per_shard, period):
                    total = total + src[i, :, lanes].astype(F32)
                acc = [acc[a] + total * coef[a][m] for a in range(pairs)]
            for a in range(pairs):
                dst[a, :, lanes] = acc[a]

    loads[0].wait()
    fold(wbuf.at[0], wsend)
    w_copy = remote(wsend, wrecv, w_sem.at[0], w_sem.at[1], core)
    w_copy.start()
    loads[1].wait()
    fold(wbuf.at[1], wown)
    for a in range(pairs):
        xr = x_rows[...].astype(F32)
        scaled[a] = jnp.concatenate(
            [xr * occ[a : a + 1, :], xr * occ[tau_count - 1 - a : tau_count - a, :]], axis=0
        ).astype(BF16)
    loads[2].wait()
    w_copy.wait_recv()

    def green(a):
        @pl.loop(0, Q // QBLOCK)
        def _(b):
            block = pl.ds(pl.multiple_of(b * QBLOCK, QBLOCK), QBLOCK)
            g = lax.dot_general(
                scaled[a], xc[block, :], (((1,), (1,)), ((), ())), preferred_element_type=F32
            )
            w = wown[a, :, block] + wrecv[a, :, block]
            sig[a, :, block] = (g * jnp.concatenate([w, w], axis=0)).astype(BF16)

    def p_copy(k):
        return remote(p_send.at[k], p_recv.at[k], p_ssem.at[k], p_rsem.at[k], core)

    def x_copy(k, s):
        return remote(
            x_send.at[k, s - 1], x_recv.at[k, s - 1], x_ssem.at[k, s - 1], x_rsem.at[k, s - 1],
            {"col": lax.rem(c + s, C)},
        )

    def partial(k):
        a, m = divmod(k, parts)

        def dot(s, ff):
            off = pl.multiple_of((lax.rem(c + s, C) * 2 + ff) * owned + m * CHUNK, CHUNK)
            return jnp.dot(sig[a], xc[:, pl.ds(off, CHUNK)], preferred_element_type=F32)

        for s in range(C):
            p_send[k, s] = dot(s, 1 - f).astype(BF16)
        p_copy(k).start()
        for s in range(C):
            keep[k, s] = dot(s, f)

    def across(k):
        p_copy(k).wait_recv()
        for s in range(1, C):
            x_send[k, s - 1] = (keep[k, s] + p_recv[k, s].astype(F32)).astype(BF16)
            x_copy(k, s).start()

    def to_right(d, k):
        o = jnp.maximum(z - d, 0)
        return remote(hp.at[o, k], hp.at[o, k], z_ssem.at[0, d, k], z_rsem.at[0, d, k], {"row": jnp.minimum(z + 1, R - 1)})

    def to_left(d, k):
        o = jnp.minimum(z + d, R - 1)
        return remote(hp.at[o, k], hp.at[o, k], z_ssem.at[1, d, k], z_rsem.at[1, d, k], {"row": jnp.maximum(z - 1, 0)})

    def from_left(d, k):
        o = jnp.maximum(z - d, 0)
        return remote(hp.at[o, k], hp.at[o, k], z_ssem.at[0, d - 1, k], z_rsem.at[0, d - 1, k], {"row": jnp.minimum(z + 1, R - 1)})

    def from_right(d, k):
        o = jnp.minimum(z + d, R - 1)
        return remote(hp.at[o, k], hp.at[o, k], z_ssem.at[1, d - 1, k], z_rsem.at[1, d - 1, k], {"row": jnp.maximum(z - 1, 0)})

    scale = 1.0 / math.sqrt(2.0 * C * Q)

    def finish(k):
        total = keep[k, 0] + p_recv[k, 0].astype(F32)
        for s in range(1, C):
            x_copy(k, s).wait_recv()
            total = total + x_recv[k, s - 1].astype(F32)
        hp[z, k] = (total * scale).astype(BF16)

        @pl.when(z < R - 1)
        def _():
            to_right(0, k).start()

        @pl.when(z > 0)
        def _():
            to_left(0, k).start()

    for k in range(n + 2):
        if k < n:
            if k % parts == 0:
                green(k // parts)
            partial(k)
        if 1 <= k <= n:
            across(k - 1)
        if k >= 2:
            finish(k - 2)

    own_basis.wait()

    @pl.loop(1, R)
    def _(s):
        basis_arrival(s).wait_recv()

    rbt[...] = jnp.concatenate([rb[s].astype(F32) for s in range(R)], axis=0).T.astype(BF16)

    @pl.loop(1, R)
    def _(d):
        for k in range(n):
            @pl.when(z - d >= 0)
            def _():
                from_left(d, k).wait_recv()

                @pl.when(z < R - 1)
                def _():
                    to_right(d, k).start()

            @pl.when(z + d <= R - 1)
            def _():
                from_right(d, k).wait_recv()

                @pl.when(z > 0)
                def _():
                    to_left(d, k).start()

    w_copy.wait_send()
    for k in range(n):
        p_copy(k).wait_send()
        for s in range(1, C):
            x_copy(k, s).wait_send()

    @pl.loop(1, R)
    def _(s):
        basis_copy(s).wait_send()

    @pl.loop(0, R)
    def _(d):
        for k in range(n):
            @pl.when((z - d >= 0) & (z < R - 1))
            def _():
                to_right(d, k).wait_send()

            @pl.when((z + d <= R - 1) & (z > 0))
            def _():
                to_left(d, k).wait_send()


def project_kernel(rows_axis, tau_count, ichunk, hp, rbt, out):
    R = rows_axis
    t = pl.program_id(0)
    z = lax.axis_index("row")
    parts = hp.shape[1] // (tau_count // 2)
    rows = hp.shape[2] // 2
    a = jnp.minimum(t, tau_count - 1 - t)
    upper = t >= tau_count // 2
    blocks = []
    for s in range(R):
        both = jnp.concatenate([hp[s, a * parts + m].astype(F32) for m in range(parts)], axis=1)
        blocks.append(jnp.where(upper, both[rows:], both[:rows]))
    right = jnp.concatenate(blocks, axis=0).astype(BF16)
    start = pl.multiple_of(lax.rem(z * ichunk, rbt.shape[0]), min(ichunk, rbt.shape[0]))
    left = rbt[...] if ichunk == rbt.shape[0] else rbt[pl.ds(start, ichunk), :]
    out[0] = jnp.dot(left, right, preferred_element_type=F32) * (1.0 / math.sqrt(R * rows))


def local(rows_axis, cols_axis, w_freq, x_rows, x_cols, occupation):
    R, C = rows_axis, cols_axis
    per_shard, rows, wide = w_freq.shape
    tau_count, norb = occupation.shape
    Q = x_cols.shape[0]
    pairs = tau_count // 2
    owned = norb // (2 * C)
    n = pairs * (owned // CHUNK)
    ichunk = norb // R
    win = max(ichunk, 128)
    dma = pltpu.SemaphoreType.DMA
    vmem = pl.BlockSpec(memory_space=pltpu.VMEM)
    anywhere = pl.BlockSpec(memory_space=pl.ANY)
    hp, rbt = pl.pallas_call(
        functools.partial(gather_kernel, R, C, tau_count),
        out_shape=(
            jax.ShapeDtypeStruct((R, n, 2 * rows, CHUNK), BF16),
            jax.ShapeDtypeStruct((win, R * rows), BF16),
        ),
        in_specs=[vmem, vmem, anywhere, anywhere],
        out_specs=(vmem, vmem),
        scratch_shapes=[
            pltpu.VMEM((2, per_shard, rows, Q), BF16),
            pltpu.VMEM((Q, norb), BF16),
            pltpu.VMEM((pairs, rows, Q), F32),
            pltpu.VMEM((pairs, rows, Q), F32),
            pltpu.VMEM((pairs, rows, Q), F32),
            pltpu.VMEM((pairs, 2 * rows, norb), BF16),
            pltpu.VMEM((pairs, 2 * rows, Q), BF16),
            pltpu.VMEM((n, C, 2 * rows, CHUNK), BF16),
            pltpu.VMEM((n, C, 2 * rows, CHUNK), BF16),
            pltpu.VMEM((n, C, 2 * rows, CHUNK), F32),
            pltpu.VMEM((n, C - 1, 2 * rows, CHUNK), BF16),
            pltpu.VMEM((n, C - 1, 2 * rows, CHUNK), BF16),
            pltpu.VMEM((R, rows, win), BF16),
            dma((4,)),
            dma((2,)),
            dma((n,)),
            dma((n,)),
            dma((n, C - 1)),
            dma((n, C - 1)),
            dma((R,)),
            dma((R,)),
            dma((2, R, n)),
            dma((2, R, n)),
        ],
        compiler_params=pltpu.CompilerParams(
            collective_id=0, has_side_effects=True, vmem_limit_bytes=44 * 1024 * 1024
        ),
        name="gather_half",
    )(x_rows, occupation, w_freq, x_cols)
    return pl.pallas_call(
        functools.partial(project_kernel, R, tau_count, ichunk),
        grid=(tau_count,),
        out_shape=jax.ShapeDtypeStruct((tau_count, ichunk, owned), F32),
        in_specs=[
            pl.BlockSpec(hp.shape, lambda t: (0, 0, 0, 0)),
            pl.BlockSpec(rbt.shape, lambda t: (0, 0)),
        ],
        out_specs=pl.BlockSpec((1, ichunk, owned), lambda t: (t, 0, 0)),
        compiler_params=pltpu.CompilerParams(vmem_limit_bytes=48 * 1024 * 1024),
        name="project",
    )(hp, rbt)


def solution(mesh):
    assert mesh.shape["freq"] == 2
    return jax.shard_map(
        functools.partial(local, mesh.shape["row"], mesh.shape["col"]),
        mesh=mesh,
        in_specs=(
            P(("grp", "freq"), "row", "col"),
            P(("grp", "row"), None),
            P(("grp", "col", "freq"), None),
            P("grp", None),
        ),
        out_specs=P("grp", "row", ("col", "freq")),
        check_vma=False,
    )
```

```python
import functools
import math

import jax
import jax.numpy as jnp
from jax import lax
from jax.experimental import pallas as pl
from jax.experimental.pallas import tpu as pltpu
from jax.sharding import PartitionSpec as P

F32 = jnp.float32
BF16 = jnp.bfloat16
MESH = pl.DeviceIdType.MESH
CHUNK = 256
QBLOCK = 256
WPARTS = 2
GATHER_VMEM = 52 * 1024 * 1024
PROJECT_VMEM = 40 * 1024 * 1024


def remote(src, dst, send_sem, recv_sem, device):
    return pltpu.make_async_remote_copy(
        src_ref=src, dst_ref=dst, send_sem=send_sem, recv_sem=recv_sem,
        device_id=device, device_id_type=MESH,
    )


def coefficients(f, shards, per_shard, tau_count, extra):
    period = tau_count + 1
    norm = extra / math.sqrt(2.0 * shards * per_shard)

    def pick(values):
        out = jnp.float32(values[0])
        for s in range(1, shards):
            out = jnp.where(f == s, jnp.float32(values[s]), out)
        return out

    coef = [
        [
            pick([
                2.0 * norm * math.cos(2.0 * math.pi * (((a + 1) * (s * per_shard + m)) % period) / period)
                for s in range(shards)
            ])
            for m in range(period)
        ]
        for a in range(tau_count // 2)
    ]
    drop = pick([norm if s == 0 else 0.0 for s in range(shards)])
    return coef, drop


def gather_kernel(
    rows_axis, cols_axis, tau_count, xr_hbm, occ_hbm, w_hbm, xc_hbm, hp, rbt,
    x_rows, occ, wbuf, xc, wsend, wown, wrecv, scaled, gbuf, sig, p_send, p_recv, keep, x_send, x_recv, rb,
    lsem, w_ssem, w_rsem, p_ssem, p_rsem, x_ssem, x_rsem, b_ssem, b_rsem, z_ssem, z_rsem,
):
    R, C = rows_axis, cols_axis
    z, c, f = lax.axis_index("row"), lax.axis_index("col"), lax.axis_index("freq")
    pairs = tau_count // 2
    rows, norb = x_rows.shape
    per_shard = w_hbm.shape[0]
    Q = xc.shape[0]
    owned = norb // (2 * C)
    parts = owned // CHUNK
    n = pairs * parts
    shares = rb.shape[0]
    win = rb.shape[3] * shares
    half = Q // WPARTS
    ichunk = norb // R
    core = {"freq": 1 - f}

    def w_load(h, q):
        owner = 1 - f if h == 0 else f
        lanes = pl.ds(pl.multiple_of(owner * Q + q * half, 128), half)
        return pltpu.make_async_copy(w_hbm.at[:, :, lanes], wbuf.at[h, q], lsem.at[h * WPARTS + q])

    rows_load = pltpu.make_async_copy(xr_hbm, x_rows, lsem.at[2 * WPARTS])
    occ_load = pltpu.make_async_copy(occ_hbm, occ, lsem.at[2 * WPARTS + 1])
    xc_load = pltpu.make_async_copy(xc_hbm, xc, lsem.at[2 * WPARTS + 2])
    rows_load.start()
    occ_load.start()
    for q in range(WPARTS):
        w_load(0, q).start()
    for q in range(WPARTS):
        w_load(1, q).start()
    xc_load.start()

    barrier = pltpu.get_barrier_semaphore()
    pl.semaphore_signal(barrier, inc=1, device_id=core, device_id_type=MESH)
    for s in range(1, C):
        pl.semaphore_signal(barrier, inc=1, device_id={"col": lax.rem(c + s, C)}, device_id_type=MESH)

    @pl.loop(1, R)
    def _(s):
        pl.semaphore_signal(barrier, inc=1, device_id={"row": lax.rem(z + s, R)}, device_id_type=MESH)

    pl.semaphore_wait(barrier, 1 + (C - 1) + (R - 1))

    rows_load.wait()
    piece = win // shares
    mine = f if shares == 2 else 0

    def window(to):
        start = (to * ichunk) // win * win + mine * piece
        return pl.ds(pl.multiple_of(start, 128), piece)

    def basis_copy(s):
        to = lax.rem(z + s, R)
        return remote(x_rows.at[:, window(to)], rb.at[mine, z], b_ssem.at[s], b_rsem.at[s], {"row": to})

    def basis_arrival(s):
        return remote(
            x_rows.at[:, window(z)], rb.at[mine, lax.rem(z - s + R, R)], b_ssem.at[s], b_rsem.at[s],
            {"row": lax.rem(z + s, R)},
        )

    @pl.loop(1, R)
    def _(s):
        basis_copy(s).start()

    own_basis = pltpu.make_async_copy(x_rows.at[:, window(z)], rb.at[mine, z], lsem.at[2 * WPARTS + 3])
    own_basis.start()

    def basis_share(which):
        return remote(rb.at[which], rb.at[which], b_ssem.at[0], b_rsem.at[0], core)

    def basis_gathered():
        own_basis.wait()

        @pl.loop(1, R)
        def _(s):
            basis_arrival(s).wait_recv()

        if shares == 2:
            basis_share(mine).start()

    def basis_done():
        if shares == 2:
            basis_share(1 - mine).wait_recv()
        sides = [
            jnp.concatenate([rb[h, s].astype(F32) for s in range(R)], axis=0) for h in range(shares)
        ]
        for h in range(shares):
            rbt[h * piece : (h + 1) * piece, :] = sides[h].T.astype(BF16)

    coef, drop = coefficients(f, 2, per_shard, tau_count, 1.0 / math.sqrt(norb))
    period = tau_count + 1

    def fold(src, dst):
        @pl.loop(0, half // 128)
        def _(b):
            lanes = pl.ds(pl.multiple_of(b * 128, 128), 128)
            first = src[0, :, lanes].astype(F32)
            acc = [first * (-drop)] * pairs
            for m in range(period):
                total = first if m == 0 else src[m, :, lanes].astype(F32)
                for i in range(m + period, per_shard, period):
                    total = total + src[i, :, lanes].astype(F32)
                acc = [acc[a] + total * coef[a][m] for a in range(pairs)]
            for a in range(pairs):
                dst[a, :, lanes] = acc[a]

    def w_copy(q):
        return remote(wsend.at[q], wrecv.at[q], w_ssem.at[q], w_rsem.at[q], core)

    for q in range(WPARTS):
        w_load(0, q).wait()
        fold(wbuf.at[0, q], wsend.at[q])
        w_copy(q).start()
    occ_load.wait()

    def scale_rows(a):
        xr = x_rows[...].astype(F32)
        scaled[a] = jnp.concatenate(
            [xr * occ[a : a + 1, :], xr * occ[tau_count - 1 - a : tau_count - a, :]], axis=0
        ).astype(BF16)

    scale_rows(0)
    for q in range(WPARTS):
        w_load(1, q).wait()
        fold(wbuf.at[1, q], wown.at[q])
    for a in range(1, pairs):
        scale_rows(a)
    xc_load.wait()

    def green(a):
        for b in range(Q // QBLOCK):
            block = pl.ds(b * QBLOCK, QBLOCK)
            gbuf[:, block] = lax.dot_general(
                scaled[a], xc[block, :], (((1,), (1,)), ((), ())), preferred_element_type=F32
            )

    def weigh(a):
        for q in range(WPARTS):
            if a == 0:
                w_copy(q).wait_recv()
            w = wown[q, a] + wrecv[q, a]
            block = pl.ds(q * half, half)
            sig[a, :, block] = (gbuf[:, block] * jnp.concatenate([w, w], axis=0)).astype(BF16)

    def p_copy(k, s):
        return remote(p_send.at[k, s], p_recv.at[k, s], p_ssem.at[k, s], p_rsem.at[k, s], core)

    def x_copy(k, s):
        return remote(
            x_send.at[k, s - 1], x_recv.at[k, s - 1], x_ssem.at[k, s - 1], x_rsem.at[k, s - 1],
            {"col": lax.rem(c + s, C)},
        )

    order = list(range(1, C)) + [0]

    def partial(k):
        a, m = divmod(k, parts)

        def dot(s, ff):
            off = pl.multiple_of((lax.rem(c + s, C) * 2 + ff) * owned + m * CHUNK, CHUNK)
            return jnp.dot(sig[a], xc[:, pl.ds(off, CHUNK)], preferred_element_type=F32)

        for s in order:
            p_send[k, s] = dot(s, 1 - f).astype(BF16)
            p_copy(k, s).start()
        for s in order:
            keep[k, s] = dot(s, f)

    def across(k):
        for s in range(1, C):
            p_copy(k, s).wait_recv()
            x_send[k, s - 1] = (keep[k, s] + p_recv[k, s].astype(F32)).astype(BF16)
            x_copy(k, s).start()

    def to_right(d, k):
        o = jnp.maximum(z - d, 0)
        return remote(hp.at[o, k], hp.at[o, k], z_ssem.at[0, d, k], z_rsem.at[0, d, k], {"row": jnp.minimum(z + 1, R - 1)})

    def to_left(d, k):
        o = jnp.minimum(z + d, R - 1)
        return remote(hp.at[o, k], hp.at[o, k], z_ssem.at[1, d, k], z_rsem.at[1, d, k], {"row": jnp.maximum(z - 1, 0)})

    def from_left(d, k):
        o = jnp.maximum(z - d, 0)
        return remote(hp.at[o, k], hp.at[o, k], z_ssem.at[0, d - 1, k], z_rsem.at[0, d - 1, k], {"row": jnp.minimum(z + 1, R - 1)})

    def from_right(d, k):
        o = jnp.minimum(z + d, R - 1)
        return remote(hp.at[o, k], hp.at[o, k], z_ssem.at[1, d - 1, k], z_rsem.at[1, d - 1, k], {"row": jnp.maximum(z - 1, 0)})

    scale = 1.0 / math.sqrt(2.0 * C * Q)

    def finish(k):
        p_copy(k, 0).wait_recv()
        total = keep[k, 0] + p_recv[k, 0].astype(F32)
        for s in range(1, C):
            x_copy(k, s).wait_recv()
            total = total + x_recv[k, s - 1].astype(F32)
        hp[z, k] = (total * scale).astype(BF16)

        @pl.when(z < R - 1)
        def _():
            to_right(0, k).start()

        @pl.when(z > 0)
        def _():
            to_left(0, k).start()

    def forward(d, k):
        @pl.when(z - d >= 0)
        def _():
            from_left(d, k).wait_recv()

            @pl.when(z < R - 1)
            def _():
                to_right(d, k).start()

        @pl.when(z + d <= R - 1)
        def _():
            from_right(d, k).wait_recv()

            @pl.when(z > 0)
            def _():
                to_left(d, k).start()

    for k in range(n + 2):
        if k < n:
            if k == 0:
                green(0)
                weigh(0)
            partial(k)
        if 1 <= k <= n:
            across(k - 1)
        if k % parts == parts - 1 and k + 1 < n:
            green((k + 1) // parts)
            weigh((k + 1) // parts)
        if k >= 2:
            finish(k - 2)
        if k == 2:
            basis_gathered()
    if n < 2:
        basis_gathered()
    basis_done()

    @pl.loop(1, R)
    def _(d):
        for k in range(n):
            forward(d, k)

    for q in range(WPARTS):
        w_copy(q).wait_send()
    if shares == 2:
        basis_share(mine).wait_send()
    for k in range(n):
        for s in range(C):
            p_copy(k, s).wait_send()
        for s in range(1, C):
            x_copy(k, s).wait_send()

    @pl.loop(1, R)
    def _(s):
        basis_copy(s).wait_send()

    @pl.loop(0, R)
    def _(d):
        for k in range(n):
            @pl.when((z - d >= 0) & (z < R - 1))
            def _():
                to_right(d, k).wait_send()

            @pl.when((z + d <= R - 1) & (z > 0))
            def _():
                to_left(d, k).wait_send()


def project_kernel(rows_axis, tau_count, ichunk, hp, rbt, out, obuf, sems):
    R = rows_axis
    z = lax.axis_index("row")
    pairs = tau_count // 2
    parts = hp.shape[1] // pairs
    rows = hp.shape[2] // 2
    start = pl.multiple_of(lax.rem(z * ichunk, rbt.shape[0]), min(ichunk, rbt.shape[0]))
    left = rbt[...] if ichunk == rbt.shape[0] else rbt[pl.ds(start, ichunk), :]
    scale = 1.0 / math.sqrt(R * rows)
    copies = []
    for a in range(pairs):
        both = [
            jnp.concatenate([hp[s, a * parts + m].astype(F32) for m in range(parts)], axis=1) for s in range(R)
        ]
        for t, first in ((a, 0), (tau_count - 1 - a, rows)):
            right = jnp.concatenate([b[first : first + rows] for b in both], axis=0).astype(BF16)
            for h in range(2):
                part = slice(h * ichunk // 2, (h + 1) * ichunk // 2)
                obuf[t, part, :] = jnp.dot(left[part], right, preferred_element_type=F32) * scale
                copies.append(pltpu.make_async_copy(obuf.at[t, part], out.at[t, part], sems.at[t, h]))
                copies[-1].start()
    for copy in copies:
        copy.wait()


def local(rows_axis, cols_axis, w_freq, x_rows, x_cols, occupation):
    R, C = rows_axis, cols_axis
    per_shard, rows, wide = w_freq.shape
    tau_count, norb = occupation.shape
    Q = x_cols.shape[0]
    pairs = tau_count // 2
    owned = norb // (2 * C)
    n = pairs * (owned // CHUNK)
    ichunk = norb // R
    win = max(ichunk, 128)
    shares = 2 if win % 256 == 0 else 1
    half = Q // WPARTS
    dma = pltpu.SemaphoreType.DMA
    vmem = pl.BlockSpec(memory_space=pltpu.VMEM)
    anywhere = pl.BlockSpec(memory_space=pl.ANY)
    hp, rbt = pl.pallas_call(
        functools.partial(gather_kernel, R, C, tau_count),
        out_shape=(
            jax.ShapeDtypeStruct((R, n, 2 * rows, CHUNK), BF16),
            jax.ShapeDtypeStruct((win, R * rows), BF16),
        ),
        in_specs=[anywhere] * 4,
        out_specs=(vmem, vmem),
        scratch_shapes=[
            pltpu.VMEM((rows, norb), BF16),
            pltpu.VMEM((tau_count, norb), F32),
            pltpu.VMEM((2, WPARTS, per_shard, rows, half), BF16),
            pltpu.VMEM((Q, norb), BF16),
            pltpu.VMEM((WPARTS, pairs, rows, half), F32),
            pltpu.VMEM((WPARTS, pairs, rows, half), F32),
            pltpu.VMEM((WPARTS, pairs, rows, half), F32),
            pltpu.VMEM((pairs, 2 * rows, norb), BF16),
            pltpu.VMEM((2 * rows, Q), F32),
            pltpu.VMEM((pairs, 2 * rows, Q), BF16),
            pltpu.VMEM((n, C, 2 * rows, CHUNK), BF16),
            pltpu.VMEM((n, C, 2 * rows, CHUNK), BF16),
            pltpu.VMEM((n, C, 2 * rows, CHUNK), F32),
            pltpu.VMEM((n, C - 1, 2 * rows, CHUNK), BF16),
            pltpu.VMEM((n, C - 1, 2 * rows, CHUNK), BF16),
            pltpu.VMEM((shares, R, rows, win // shares), BF16),
            dma((2 * WPARTS + 4,)),
            dma((WPARTS,)),
            dma((WPARTS,)),
            dma((n, C)),
            dma((n, C)),
            dma((n, C - 1)),
            dma((n, C - 1)),
            dma((R,)),
            dma((R,)),
            dma((2, R, n)),
            dma((2, R, n)),
        ],
        compiler_params=pltpu.CompilerParams(
            collective_id=0, has_side_effects=True, vmem_limit_bytes=GATHER_VMEM
        ),
        name="gather_half",
    )(x_rows, occupation, w_freq, x_cols)
    return pl.pallas_call(
        functools.partial(project_kernel, R, tau_count, ichunk),
        out_shape=jax.ShapeDtypeStruct((tau_count, ichunk, owned), F32),
        in_specs=[vmem, vmem],
        out_specs=anywhere,
        scratch_shapes=[pltpu.VMEM((tau_count, ichunk, owned), F32), dma((tau_count, 2))],
        compiler_params=pltpu.CompilerParams(vmem_limit_bytes=PROJECT_VMEM),
        name="project",
    )(hp, rbt)


def solution(mesh):
    assert mesh.shape["freq"] == 2
    return jax.shard_map(
        functools.partial(local, mesh.shape["row"], mesh.shape["col"]),
        mesh=mesh,
        in_specs=(
            P(("grp", "freq"), "row", "col"),
            P(("grp", "row"), None),
            P(("grp", "col", "freq"), None),
            P("grp", None),
        ),
        out_specs=P("grp", "row", ("col", "freq")),
        check_vma=False,
    )
```

```python
import functools
import math

import jax
import jax.numpy as jnp
from jax import lax
from jax.experimental import pallas as pl
from jax.experimental.pallas import tpu as pltpu
from jax.sharding import PartitionSpec as P

F32 = jnp.float32
BF16 = jnp.bfloat16
MESH = pl.DeviceIdType.MESH
CHUNK = 256
QBLOCK = 256
WPARTS = 2
AHEAD = 1
GATHER_VMEM = 52 * 1024 * 1024
PROJECT_VMEM = 40 * 1024 * 1024


def remote(src, dst, send_sem, recv_sem, device):
    return pltpu.make_async_remote_copy(
        src_ref=src, dst_ref=dst, send_sem=send_sem, recv_sem=recv_sem,
        device_id=device, device_id_type=MESH,
    )


def coefficients(f, shards, per_shard, tau_count, extra):
    period = tau_count + 1
    norm = extra / math.sqrt(2.0 * shards * per_shard)

    def pick(values):
        out = jnp.float32(values[0])
        for s in range(1, shards):
            out = jnp.where(f == s, jnp.float32(values[s]), out)
        return out

    coef = [
        [
            pick([
                2.0 * norm * math.cos(2.0 * math.pi * (((a + 1) * (s * per_shard + m)) % period) / period)
                for s in range(shards)
            ])
            for m in range(period)
        ]
        for a in range(tau_count // 2)
    ]
    drop = pick([norm if s == 0 else 0.0 for s in range(shards)])
    return coef, drop


def gather_kernel(
    rows_axis, cols_axis, tau_count, xr_hbm, occ_hbm, w_hbm, xc_hbm, hp, rbt,
    x_rows, occ, wbuf, xc, wsend, wown, wrecv, scaled, gbuf, sig, p_send, p_recv, keep, x_send, x_recv, rb,
    lsem, w_ssem, w_rsem, p_ssem, p_rsem, x_ssem, x_rsem, b_ssem, b_rsem, z_ssem, z_rsem,
):
    R, C = rows_axis, cols_axis
    z, c, f = lax.axis_index("row"), lax.axis_index("col"), lax.axis_index("freq")
    pairs = tau_count // 2
    rows, norb = x_rows.shape
    per_shard = w_hbm.shape[0]
    Q = xc.shape[0]
    owned = norb // (2 * C)
    parts = owned // CHUNK
    n = pairs * parts
    shares = rb.shape[0]
    win = rb.shape[3] * shares
    half = Q // WPARTS
    ichunk = norb // R
    core = {"freq": 1 - f}

    def w_load(h, q):
        owner = 1 - f if h == 0 else f
        lanes = pl.ds(pl.multiple_of(owner * Q + q * half, 128), half)
        return pltpu.make_async_copy(w_hbm.at[:, :, lanes], wbuf.at[h, q], lsem.at[h * WPARTS + q])

    rows_load = pltpu.make_async_copy(xr_hbm, x_rows, lsem.at[2 * WPARTS])
    occ_load = pltpu.make_async_copy(occ_hbm, occ, lsem.at[2 * WPARTS + 1])
    xc_load = pltpu.make_async_copy(xc_hbm, xc, lsem.at[2 * WPARTS + 2])
    rows_load.start()
    occ_load.start()
    for q in range(WPARTS):
        w_load(0, q).start()
    for q in range(WPARTS):
        w_load(1, q).start()
    xc_load.start()

    barrier = pltpu.get_barrier_semaphore()
    pl.semaphore_signal(barrier, inc=1, device_id=core, device_id_type=MESH)
    for s in range(1, C):
        pl.semaphore_signal(barrier, inc=1, device_id={"col": lax.rem(c + s, C)}, device_id_type=MESH)

    @pl.loop(1, R)
    def _(s):
        pl.semaphore_signal(barrier, inc=1, device_id={"row": lax.rem(z + s, R)}, device_id_type=MESH)

    pl.semaphore_wait(barrier, 1 + (C - 1) + (R - 1))

    rows_load.wait()
    piece = win // shares
    mine = f if shares == 2 else 0

    def window(to):
        start = (to * ichunk) // win * win + mine * piece
        return pl.ds(pl.multiple_of(start, 128), piece)

    def basis_copy(s):
        to = lax.rem(z + s, R)
        return remote(x_rows.at[:, window(to)], rb.at[mine, z], b_ssem.at[s], b_rsem.at[s], {"row": to})

    def basis_arrival(s):
        return remote(
            x_rows.at[:, window(z)], rb.at[mine, lax.rem(z - s + R, R)], b_ssem.at[s], b_rsem.at[s],
            {"row": lax.rem(z + s, R)},
        )

    @pl.loop(1, R)
    def _(s):
        basis_copy(s).start()

    own_basis = pltpu.make_async_copy(x_rows.at[:, window(z)], rb.at[mine, z], lsem.at[2 * WPARTS + 3])
    own_basis.start()

    def basis_share(which):
        return remote(rb.at[which], rb.at[which], b_ssem.at[0], b_rsem.at[0], core)

    def basis_gathered():
        own_basis.wait()

        @pl.loop(1, R)
        def _(s):
            basis_arrival(s).wait_recv()

        if shares == 2:
            basis_share(mine).start()

    def basis_done():
        if shares == 2:
            basis_share(1 - mine).wait_recv()
        sides = [
            jnp.concatenate([rb[h, s].astype(F32) for s in range(R)], axis=0) for h in range(shares)
        ]
        for h in range(shares):
            rbt[h * piece : (h + 1) * piece, :] = sides[h].T.astype(BF16)

    coef, drop = coefficients(f, 2, per_shard, tau_count, 1.0 / math.sqrt(norb))
    period = tau_count + 1

    def fold(src, dst):
        @pl.loop(0, half // 128)
        def _(b):
            lanes = pl.ds(pl.multiple_of(b * 128, 128), 128)
            first = src[0, :, lanes].astype(F32)
            acc = [first * (-drop)] * pairs
            for m in range(period):
                total = first if m == 0 else src[m, :, lanes].astype(F32)
                for i in range(m + period, per_shard, period):
                    total = total + src[i, :, lanes].astype(F32)
                acc = [acc[a] + total * coef[a][m] for a in range(pairs)]
            for a in range(pairs):
                dst[a, :, lanes] = acc[a]

    def w_copy(q):
        return remote(wsend.at[q], wrecv.at[q], w_ssem.at[q], w_rsem.at[q], core)

    for q in range(WPARTS):
        w_load(0, q).wait()
        fold(wbuf.at[0, q], wsend.at[q])
        w_copy(q).start()
    occ_load.wait()

    def scale_rows(a):
        xr = x_rows[...].astype(F32)
        scaled[a] = jnp.concatenate(
            [xr * occ[a : a + 1, :], xr * occ[tau_count - 1 - a : tau_count - a, :]], axis=0
        ).astype(BF16)

    scale_rows(0)
    for q in range(WPARTS):
        w_load(1, q).wait()
        fold(wbuf.at[1, q], wown.at[q])
    for a in range(1, pairs):
        scale_rows(a)
    xc_load.wait()

    def green(a):
        for b in range(Q // QBLOCK):
            block = pl.ds(b * QBLOCK, QBLOCK)
            gbuf[:, block] = lax.dot_general(
                scaled[a], xc[block, :], (((1,), (1,)), ((), ())), preferred_element_type=F32
            )

    def weigh(a):
        for q in range(WPARTS):
            if a == 0:
                w_copy(q).wait_recv()
            w = wown[q, a] + wrecv[q, a]
            block = pl.ds(q * half, half)
            sig[a, :, block] = (gbuf[:, block] * jnp.concatenate([w, w], axis=0)).astype(BF16)

    def p_copy(k, s):
        return remote(p_send.at[k, s], p_recv.at[k, s], p_ssem.at[k, s], p_rsem.at[k, s], core)

    def x_copy(k, s):
        return remote(
            x_send.at[k, s - 1], x_recv.at[k, s - 1], x_ssem.at[k, s - 1], x_rsem.at[k, s - 1],
            {"col": lax.rem(c + s, C)},
        )

    order = list(range(1, C)) + [0]

    def partial(k):
        a, m = divmod(k, parts)

        def dot(s, ff):
            off = pl.multiple_of((lax.rem(c + s, C) * 2 + ff) * owned + m * CHUNK, CHUNK)
            return jnp.dot(sig[a], xc[:, pl.ds(off, CHUNK)], preferred_element_type=F32)

        for s in order:
            p_send[k, s] = dot(s, 1 - f).astype(BF16)
            p_copy(k, s).start()
        for s in order:
            keep[k, s] = dot(s, f)

    def across(k):
        for s in range(1, C):
            p_copy(k, s).wait_recv()
            x_send[k, s - 1] = (keep[k, s] + p_recv[k, s].astype(F32)).astype(BF16)
            x_copy(k, s).start()

    def to_right(d, k):
        o = jnp.maximum(z - d, 0)
        return remote(hp.at[o, k], hp.at[o, k], z_ssem.at[0, d, k], z_rsem.at[0, d, k], {"row": jnp.minimum(z + 1, R - 1)})

    def to_left(d, k):
        o = jnp.minimum(z + d, R - 1)
        return remote(hp.at[o, k], hp.at[o, k], z_ssem.at[1, d, k], z_rsem.at[1, d, k], {"row": jnp.maximum(z - 1, 0)})

    def from_left(d, k):
        o = jnp.maximum(z - d, 0)
        return remote(hp.at[o, k], hp.at[o, k], z_ssem.at[0, d - 1, k], z_rsem.at[0, d - 1, k], {"row": jnp.minimum(z + 1, R - 1)})

    def from_right(d, k):
        o = jnp.minimum(z + d, R - 1)
        return remote(hp.at[o, k], hp.at[o, k], z_ssem.at[1, d - 1, k], z_rsem.at[1, d - 1, k], {"row": jnp.maximum(z - 1, 0)})

    scale = 1.0 / math.sqrt(2.0 * C * Q)

    def finish(k):
        p_copy(k, 0).wait_recv()
        total = keep[k, 0] + p_recv[k, 0].astype(F32)
        for s in range(1, C):
            x_copy(k, s).wait_recv()
            total = total + x_recv[k, s - 1].astype(F32)
        hp[z, k] = (total * scale).astype(BF16)

        @pl.when(z < R - 1)
        def _():
            to_right(0, k).start()

        @pl.when(z > 0)
        def _():
            to_left(0, k).start()

    def forward(d, k):
        @pl.when(z - d >= 0)
        def _():
            from_left(d, k).wait_recv()

            @pl.when(z < R - 1)
            def _():
                to_right(d, k).start()

        @pl.when(z + d <= R - 1)
        def _():
            from_right(d, k).wait_recv()

            @pl.when(z > 0)
            def _():
                to_left(d, k).start()

    for k in range(n + 2):
        if k < n:
            if k == 0:
                green(0)
                weigh(0)
            partial(k)
        if 1 <= k <= n:
            across(k - 1)
        if k % parts == parts - 1 and k + 1 < n:
            green((k + 1) // parts)
            weigh((k + 1) // parts)
        if k >= 2:
            finish(k - 2)
        if k >= 2 + AHEAD and R > 1:
            forward(1, k - 2 - AHEAD)
        if k == 2:
            basis_gathered()
    if n < 2:
        basis_gathered()
    basis_done()

    for k in range(max(n - AHEAD, 0), n):
        if R > 1:
            forward(1, k)

    @pl.loop(2, R)
    def _(d):
        for k in range(n):
            forward(d, k)

    for q in range(WPARTS):
        w_copy(q).wait_send()
    if shares == 2:
        basis_share(mine).wait_send()
    for k in range(n):
        for s in range(C):
            p_copy(k, s).wait_send()
        for s in range(1, C):
            x_copy(k, s).wait_send()

    @pl.loop(1, R)
    def _(s):
        basis_copy(s).wait_send()

    @pl.loop(0, R)
    def _(d):
        for k in range(n):
            @pl.when((z - d >= 0) & (z < R - 1))
            def _():
                to_right(d, k).wait_send()

            @pl.when((z + d <= R - 1) & (z > 0))
            def _():
                to_left(d, k).wait_send()


def project_kernel(rows_axis, tau_count, ichunk, hp, rbt, out, obuf, sems):
    R = rows_axis
    z = lax.axis_index("row")
    pairs = tau_count // 2
    parts = hp.shape[1] // pairs
    rows = hp.shape[2] // 2
    start = pl.multiple_of(lax.rem(z * ichunk, rbt.shape[0]), min(ichunk, rbt.shape[0]))
    left = rbt[...] if ichunk == rbt.shape[0] else rbt[pl.ds(start, ichunk), :]
    scale = 1.0 / math.sqrt(R * rows)
    copies = []
    for a in range(pairs):
        both = [
            jnp.concatenate([hp[s, a * parts + m].astype(F32) for m in range(parts)], axis=1) for s in range(R)
        ]
        for t, first in ((a, 0), (tau_count - 1 - a, rows)):
            right = jnp.concatenate([b[first : first + rows] for b in both], axis=0).astype(BF16)
            for h in range(2):
                part = slice(h * ichunk // 2, (h + 1) * ichunk // 2)
                obuf[t, part, :] = jnp.dot(left[part], right, preferred_element_type=F32) * scale
                copies.append(pltpu.make_async_copy(obuf.at[t, part], out.at[t, part], sems.at[t, h]))
                copies[-1].start()
    for copy in copies:
        copy.wait()


def local(rows_axis, cols_axis, w_freq, x_rows, x_cols, occupation):
    R, C = rows_axis, cols_axis
    per_shard, rows, wide = w_freq.shape
    tau_count, norb = occupation.shape
    Q = x_cols.shape[0]
    pairs = tau_count // 2
    owned = norb // (2 * C)
    n = pairs * (owned // CHUNK)
    ichunk = norb // R
    win = max(ichunk, 128)
    shares = 2 if win % 256 == 0 else 1
    half = Q // WPARTS
    dma = pltpu.SemaphoreType.DMA
    vmem = pl.BlockSpec(memory_space=pltpu.VMEM)
    anywhere = pl.BlockSpec(memory_space=pl.ANY)
    hp, rbt = pl.pallas_call(
        functools.partial(gather_kernel, R, C, tau_count),
        out_shape=(
            jax.ShapeDtypeStruct((R, n, 2 * rows, CHUNK), BF16),
            jax.ShapeDtypeStruct((win, R * rows), BF16),
        ),
        in_specs=[anywhere] * 4,
        out_specs=(vmem, vmem),
        scratch_shapes=[
            pltpu.VMEM((rows, norb), BF16),
            pltpu.VMEM((tau_count, norb), F32),
            pltpu.VMEM((2, WPARTS, per_shard, rows, half), BF16),
            pltpu.VMEM((Q, norb), BF16),
            pltpu.VMEM((WPARTS, pairs, rows, half), F32),
            pltpu.VMEM((WPARTS, pairs, rows, half), F32),
            pltpu.VMEM((WPARTS, pairs, rows, half), F32),
            pltpu.VMEM((pairs, 2 * rows, norb), BF16),
            pltpu.VMEM((2 * rows, Q), F32),
            pltpu.VMEM((pairs, 2 * rows, Q), BF16),
            pltpu.VMEM((n, C, 2 * rows, CHUNK), BF16),
            pltpu.VMEM((n, C, 2 * rows, CHUNK), BF16),
            pltpu.VMEM((n, C, 2 * rows, CHUNK), F32),
            pltpu.VMEM((n, C - 1, 2 * rows, CHUNK), BF16),
            pltpu.VMEM((n, C - 1, 2 * rows, CHUNK), BF16),
            pltpu.VMEM((shares, R, rows, win // shares), BF16),
            dma((2 * WPARTS + 4,)),
            dma((WPARTS,)),
            dma((WPARTS,)),
            dma((n, C)),
            dma((n, C)),
            dma((n, C - 1)),
            dma((n, C - 1)),
            dma((R,)),
            dma((R,)),
            dma((2, R, n)),
            dma((2, R, n)),
        ],
        compiler_params=pltpu.CompilerParams(
            collective_id=0, has_side_effects=True, vmem_limit_bytes=GATHER_VMEM
        ),
        name="gather_half",
    )(x_rows, occupation, w_freq, x_cols)
    return pl.pallas_call(
        functools.partial(project_kernel, R, tau_count, ichunk),
        out_shape=jax.ShapeDtypeStruct((tau_count, ichunk, owned), F32),
        in_specs=[vmem, vmem],
        out_specs=anywhere,
        scratch_shapes=[pltpu.VMEM((tau_count, ichunk, owned), F32), dma((tau_count, 2))],
        compiler_params=pltpu.CompilerParams(vmem_limit_bytes=PROJECT_VMEM),
        name="project",
    )(hp, rbt)


def solution(mesh):
    assert mesh.shape["freq"] == 2
    return jax.shard_map(
        functools.partial(local, mesh.shape["row"], mesh.shape["col"]),
        mesh=mesh,
        in_specs=(
            P(("grp", "freq"), "row", "col"),
            P(("grp", "row"), None),
            P(("grp", "col", "freq"), None),
            P("grp", None),
        ),
        out_specs=P("grp", "row", ("col", "freq")),
        check_vma=False,
    )
```
